128 devices in a mesh: dp: 16 (over y_lo, z, core), mp: 8 (over y_hi, x).
Axes of the slice: x: 4, y: 4 (y_hi: 2, y_lo: 2; y = y_hi * 2 + y_lo), z: 4, core: 2. Of those that a mesh axis runs over, the one named last changes fastest.
Arguments:
- states: bfloat16 [16, 1024, 3072], P('dp', 'mp'), may hold values from -6 to 6
- adjoint: bfloat16 [16, 1024, 3072], P('dp', 'mp'), may hold values from -6 to 6
- step_index: int32 [16], P('dp'), may hold values from 0 to 27
- modulation: float32 [28, 3, 3072], replicated, may hold values from -3 to 3
- up_projection_weight: bfloat16 [3072, 6144], P(None, 'mp'), may hold values from -0.109375 to 0.109375
- down_projection_weight: bfloat16 [6144, 3072], P('mp'), may hold values from -0.078125 to 0.078125
- offset: bfloat16 [3072, 6144], P('dp', 'mp'), may hold values from -0.078125 to 0.078125
Outputs:
- adjoint_rate: float32 [16, 1024, 3072], P('dp', 'mp')
- offset_grad: float32 [3072, 6144], P('dp', 'mp')
The draws below stay inside these ranges and needn't reach their ends.
All inputs are finite; a program needn't handle non-finite values.
Results may differ from the reference program's by a relative error of at most 0.019.
Values may be sent and summed in bfloat16 or wider, within the bound.
A program may use at most 128 MiB of HBM per device.

```python
import math
import jax
import jax.numpy as jnp
from jax import lax

D = 3072
FF = 6144
STEPS = 28
LENGTH = 1024
SAMPLES = 16
N_MP = 8


def with_ends(drawn, rng, smallest, largest):
    shape = drawn.shape
    spot = [jax.random.randint(jax.random.fold_in(rng, axis), (), 0, shape[axis]) for axis in range(len(shape))]
    drawn = drawn.at[tuple(spot)].set(smallest)
    longest = shape.index(max(shape))
    spot[longest] = (spot[longest] + 1) % shape[longest]
    return drawn.at[tuple(spot)].set(largest)


def steps_of(stream_key, shape, pieces, least, high):
    level, own = 1.0, jax.random.fold_in(stream_key, 6)
    for dim, blocks in pieces:
        steps = jnp.exp(jax.random.uniform(jax.random.fold_in(own, dim), (blocks,), jnp.float32, least / len(pieces), high / len(pieces)))
        level = level * jnp.repeat(steps, shape[dim] // blocks).reshape([-1 if axis == dim else 1 for axis in range(len(shape))])
    return level


def centred(own_key, extent, scale, limit, cuts=(), dtype=jnp.bfloat16):
    drawn = scale * jax.random.normal(own_key, extent, jnp.float32)
    if cuts:
        drawn = drawn * steps_of(own_key, extent, cuts, -0.22, 0.18)
    return jnp.clip(drawn, -limit, limit).astype(dtype)


def setup_inputs(seed: int = 0) -> dict:
    keys = jax.random.split(jax.random.key(seed), 8)
    return {
        "states": centred(keys[0], (SAMPLES, LENGTH, D), 1.0, 6.0, ((0, 16), (1, 8))),
        "adjoint": centred(keys[1], (SAMPLES, LENGTH, D), 1.0, 6.0, ((0, 16), (1, 8))),
        "step_index": with_ends(jax.random.randint(keys[2], (SAMPLES,), 0, STEPS), jax.random.fold_in(keys[2], 1), 0, STEPS - 1).astype(jnp.int32),
        "modulation": centred(keys[3], (STEPS, 3, D), 0.5, 3.0, (), jnp.float32),
        "up_projection_weight": centred(keys[4], (D, FF), D ** -0.5, 0.109375, ((1, 8),)),
        "down_projection_weight": centred(keys[5], (FF, D), FF ** -0.5, 0.078125, ((0, 8),)),
        "offset": centred(keys[6], (D, FF), FF ** -0.5, 0.078125, ((0, 16), (1, 8))),
    }


def gelu_tanh(value):
    coeff = math.sqrt(2.0 / math.pi)
    inner = coeff * (value + 0.044715 * value * value * value)
    return 0.5 * value * (1.0 + jnp.tanh(inner))

def gelu_slope(value):
    coeff = math.sqrt(2.0 / math.pi)
    inner = coeff * (value + 0.044715 * value * value * value)
    tangent = jnp.tanh(inner)
    return 0.5 * (1.0 + tangent) + 0.5 * value * (1.0 - tangent * tangent) * coeff * (1.0 + 3.0 * 0.044715 * value * value)

def grouped_sum(left, right):
    width = FF // N_MP
    left_groups = left.astype(jnp.float32).reshape(left.shape[0], N_MP, width)
    right_groups = right.astype(jnp.float32).reshape(right.shape[0], N_MP, width)
    parts = jnp.einsum('lkf,dkf->kld', left_groups, right_groups)
    parts = parts.astype(jnp.bfloat16).astype(jnp.float32)
    return lax.optimization_barrier(jnp.sum(parts, axis=0))

def reference(states, adjoint, step_index, modulation, up_projection_weight, down_projection_weight, offset):
    rates = []
    grad_total = jnp.zeros((D, FF), jnp.float32)
    for sample in range(SAMPLES):
        mods = modulation[step_index[sample]]
        shift, scale, gate = (mods[0], mods[1], mods[2])
        timing = (step_index[sample].astype(jnp.float32) + 1.0) / (STEPS + 1.0)
        sigma = jnp.sqrt(2.0 * (1.0 - timing) / timing)
        inputs = states[sample].astype(jnp.float32)
        mean = lax.optimization_barrier(jnp.mean(inputs, axis=-1, keepdims=True))
        var = lax.optimization_barrier(jnp.mean((inputs - mean) ** 2, axis=-1, keepdims=True))
        rstd = lax.rsqrt(var + 1e-06)
        normed = (inputs - mean) * rstd
        modulated_input = (normed * (1.0 + scale) + shift).astype(jnp.bfloat16)
        hidden_features = jnp.dot(modulated_input, up_projection_weight, preferred_element_type=jnp.float32)
        activation_output = gelu_tanh(hidden_features).astype(jnp.bfloat16)
        adj = adjoint[sample].astype(jnp.float32)
        gated_output = (adj * gate).astype(jnp.bfloat16)
        activation_gradient = jnp.dot(gated_output, down_projection_weight.T, preferred_element_type=jnp.float32)
        hidden_gradient = (activation_gradient * gelu_slope(hidden_features)).astype(jnp.bfloat16)
        grad_mod = grouped_sum(hidden_gradient, up_projection_weight)
        scaled = grad_mod * (1.0 + scale)
        rate = rstd * (scaled - lax.optimization_barrier(jnp.mean(scaled, axis=-1, keepdims=True)) - normed * lax.optimization_barrier(jnp.mean(scaled * normed, axis=-1, keepdims=True)))
        rates.append(rate)
        velocity_gap = grouped_sum(activation_output, offset)
        residual = 2.0 / sigma * gate * velocity_gap + sigma * adj
        weighted = (gate / sigma * residual).astype(jnp.bfloat16)
        grad_total = grad_total + jnp.dot(weighted.T, activation_output, preferred_element_type=jnp.float32)
    offset_grad = grad_total / math.sqrt(SAMPLES * LENGTH)
    return (jnp.stack(rates, axis=0), offset_grad)
```

```python
import functools
import math

import jax
import jax.numpy as jnp
from jax import lax
from jax.experimental import pallas as pl
from jax.experimental.pallas import tpu as pltpu
from jax.sharding import PartitionSpec as P

MESH = pl.DeviceIdType.MESH
BF = jnp.bfloat16
F32 = jnp.float32
D = 3072
T = 128
HH = 768
NT = (((1,), (1,)), ((), ()))
NN = (((1,), (0,)), ((), ()))
N_MSG = 80


def gelu_both(value):
    coeff = math.sqrt(2.0 / math.pi)
    square = value * value
    tangent = jnp.tanh(coeff * value * (1.0 + 0.044715 * square))
    half = 0.5 * (1.0 + tangent)
    slope = half + 0.5 * value * (1.0 - tangent * tangent) * coeff * (1.0 + 3.0 * 0.044715 * square)
    return value * half, slope


def dot(a, b, dims):
    return lax.dot_general(a, b, dims, preferred_element_type=F32)


def loop(count, body):
    def step(i, carry):
        body(i)
        return carry

    lax.fori_loop(0, count, step, 0)


def kernel(
    mod_in, gat_in, adj_in, rows_in, up_in, down_in, off_in,
    gm_out, og_out,
    modb, gatb, upb, downb, ofs, actb, slp, ghb, sopp, sun, sai, pown,
    vA, vB, vL, vR, jA, jB, jL, jR, gcore, zA, zB, zL, zR, ysum, yr,
    ss, rs, ls,
):
    dp, mp = lax.axis_index("dp"), lax.axis_index("mp")
    c, z, yl = dp % 2, (dp // 2) % 4, dp // 8
    x, yh = mp % 4, mp // 4
    y = yh * 2 + yl

    def dev(xx, yy, zz, cc):
        return (((yy % 2) * 4 + zz) * 2 + cc, (yy // 2) * 4 + xx)

    right, left = dev((x + 1) % 4, y, z, c), dev((x + 3) % 4, y, z, c)
    z_up, z_dn = (z + 1) % 4, (z + 3) % 4
    z_op = (z + 2) % 4
    zright, zleft = dev(x, y, z_up, c), dev(x, y, z_dn, c)
    y_up, y_dn, y_op = (y + 1) % 4, (y + 3) % 4, (y + 2) % 4
    yright, yleft, yfar = dev(x, y_up, z, c), dev(x, y_dn, z, c), dev(x, y_op, z, c)
    ypair = dev(x, 3 - y, z, c)
    sib = dev(x, y, z, 1 - c)
    oh = 1 - yh

    count = [0]
    unsent = {}

    def send(src, dst, device):
        i = count[0]
        count[0] += 1
        msg = pltpu.make_async_remote_copy(
            src_ref=src, dst_ref=dst, send_sem=ss.at[i], recv_sem=rs.at[i],
            device_id=device, device_id_type=MESH,
        )
        msg.start()
        unsent[id(msg)] = msg
        return msg

    def sent(*msgs):
        for m in msgs:
            m.wait_send()
            del unsent[id(m)]

    def local(i, src, dst):
        copy = pltpu.make_async_copy(src, dst, ls.at[i])
        copy.start()
        return copy

    l_up = local(0, up_in, upb.at[yh])
    l_mod = local(1, mod_in, modb.at[0])
    l_off = local(2, off_in, ofs.at[yh, yl, z, c])
    l_gat = local(3, gat_in, gatb.at[0])
    l_down = local(4, down_in, downb.at[yh])

    barrier = pltpu.get_barrier_semaphore()
    peers = (right, left, zright, zleft, yright, yleft, yfar, sib)
    for peer in peers:
        pl.semaphore_signal(barrier, inc=1, device_id=peer, device_id_type=MESH)
    pl.semaphore_wait(barrier, len(peers))

    lo, hi = pl.ds(0, T // 2), pl.ds(T // 2, T // 2)

    def xg_start(src, buf):
        return send(src, buf.at[1], right), send(src, buf.at[2], left)

    def xg_mid(buf, first):
        first[0].wait_recv()
        a = send(buf.at[1, lo], buf.at[3, lo], right)
        first[1].wait_recv()
        b = send(buf.at[2, hi], buf.at[3, hi], left)
        return a, b

    def arrived(msgs):
        for m in msgs:
            m.wait_recv()

    def rows_of(zz, cc, size, half=None):
        if half is None:
            return pl.ds((zz * 2 + cc) * size, size)
        return pl.ds((zz * 2 + cc) * size + half * (size // 2), size // 2)

    def w_start(src, buf, size):
        r = rows_of(z, c, size)
        return send(src.at[r], buf.at[yh, r], ypair)

    def w_ring(buf, size, first):
        first.wait_recv()
        piece = buf.at[oh, rows_of(z, c, size)]
        return send(piece, piece, zright), send(piece, piece, zleft), send(piece, piece, sib)

    def w_mid(buf, size, msgs):
        msgs[0].wait_recv()
        a_ref = buf.at[oh, rows_of(z_dn, c, size, 0)]
        a = send(a_ref, a_ref, zright)
        msgs[1].wait_recv()
        b_ref = buf.at[oh, rows_of(z_up, c, size, 1)]
        b = send(b_ref, b_ref, zleft)
        p, q = buf.at[oh, rows_of(z_dn, c, size)], buf.at[oh, rows_of(z_up, c, size)]
        return a, b, send(p, p, sib), send(q, q, sib)

    def w_end(buf, size, msgs):
        msgs[0].wait_recv()
        msgs[1].wait_recv()
        p = buf.at[oh, rows_of(z_op, c, size)]
        return send(p, p, sib)

    USZ, DSZ = D // 8, HH // 8

    m1 = xg_start(mod_in, modb)
    u1 = w_start(up_in, upb, USZ)
    ob = ofs.at[yh, yl, z, c]
    o1 = (send(off_in, ob, zright), send(off_in, ob, zleft))

    def p_hidden(h, row0, rows, slot0):
        slots = rows // T

        def body(j):
            cols = pl.ds(pl.multiple_of(j * 256, 256), 256)
            mod = modb[pl.ds(slot0, slots)].reshape(rows, D)
            act, slope = gelu_both(dot(mod, upb[h, :, cols], NN))
            actb[h, pl.ds(row0, rows), cols] = act.astype(BF)
            slp[h, pl.ds(row0, rows), cols] = slope

        loop(HH // 256, body)

    def p_gh(h, row0, rows, slot0):
        slots = rows // T

        def body(j):
            off = pl.multiple_of(j * 256, 256)
            cols = pl.ds(off, 256)
            gat = gatb[pl.ds(slot0, slots)].reshape(rows, D)
            grad = dot(gat, downb[h, pl.ds(off, 256), :], NT)
            ghb[h, pl.ds(row0, rows), cols] = (grad * slp[h, pl.ds(row0, rows), cols]).astype(BF)

        loop(HH // 256, body)

    l_mod.wait()
    l_up.wait()
    p_hidden(yh, 0, T, 0)

    l_off.wait()
    o1[0].wait_recv()
    hA, hB = pl.ds(0, 96), pl.ds(96, 96)
    r1 = ofs.at[yh, yl, z_dn, c, hA]
    o2a = send(r1, r1, zright)
    o1[1].wait_recv()
    r2 = ofs.at[yh, yl, z_up, c, hB]
    o2b = send(r2, r2, zleft)
    arrived((o2a, o2b))
    bundle = ofs.at[yh, yl, :, c]
    o3 = (send(bundle, bundle, yright), send(bundle, bundle, yleft), send(bundle, bundle, sib))

    u2 = w_ring(upb, USZ, u1)

    m2 = xg_mid(modb, m1)
    l_gat.wait()
    g1 = xg_start(gat_in, gatb)
    p_hidden(yh, T, 2 * T, 1)
    u3 = w_mid(upb, USZ, u2)
    arrived(m2)
    p_hidden(yh, 3 * T, T, 3)
    u4 = w_end(upb, USZ, u3)

    def ybundle(yy, half=None):
        if half is None:
            return ofs.at[yy // 2, yy % 2, :, c]
        return ofs.at[yy // 2, yy % 2, pl.ds(2 * half, 2), c]

    o3[0].wait_recv()
    r3 = ybundle(y_dn, 0)
    o4a = send(r3, r3, yright)
    o3[1].wait_recv()
    r4 = ybundle(y_up, 1)
    o4b = send(r4, r4, yleft)
    r5, r6 = ybundle(y_dn), ybundle(y_up)
    o4c, o4d = send(r5, r5, sib), send(r6, r6, sib)
    d1 = w_start(down_in, downb, DSZ)

    arrived((u2[2], u3[2], u3[3], u4))
    p_hidden(oh, 0, 4 * T, 0)

    g2 = xg_mid(gatb, g1)
    l_down.wait()
    p_gh(yh, 0, 3 * T, 0)
    arrived((o4a, o4b))
    r7 = ybundle(y_op)
    o5 = send(r7, r7, sib)
    arrived(g2)
    p_gh(yh, 3 * T, T, 3)
    arrived((o3[2], o4c, o4d, o5))
    d2 = w_ring(downb, DSZ, d1)

    def tile_sum(src, wt, rows, j):
        acc = None
        for h in range(2):
            lhs = [src[h, r, :] for r in rows]
            lhs = lhs[0] if len(lhs) == 1 else jnp.concatenate(lhs, axis=0)
            part = dot(lhs, wt(h, j), NT)
            acc = part if acc is None else acc + part
        return acc

    def cols_of(j):
        return pl.ds(pl.multiple_of(j * 384, 384), 384)

    def wt_off(h, j):
        return ofs[h, j // 4, j % 4].reshape(384, HH)

    def wt_up(h, j):
        return upb[h, pl.ds(pl.multiple_of(j * 384, 384), 384), :]

    OWN, FAR = (pl.ds(0, T),), (pl.ds(3 * T, T),)
    UNAIDED = (pl.ds(T + 64, T),)
    AIDED = (pl.ds(T, 64), pl.ds(2 * T + 64, 64))

    def rs_far(src, wt, A, B):
        def body(j):
            sopp[:, cols_of(j)] = tile_sum(src, wt, FAR, j).astype(BF)

        loop(8, body)
        return send(sopp.at[lo], A, left), send(sopp.at[hi], B, right)

    def rs_near(src, wt, fL, fR):
        def body(j):
            sun[:, cols_of(j)] = tile_sum(src, wt, UNAIDED, j).astype(BF)

        loop(8, body)
        return send(sun.at[lo], fR.at[hi], left), send(sun.at[hi], fL.at[lo], right)

    def rs_own(src, wt):
        def body(j):
            pown[:, cols_of(j)] = tile_sum(src, wt, OWN, j)

        loop(8, body)

    def rs_aided(src, wt, A, B, first, fL, fR):
        arrived(first)

        def body(j):
            acc = tile_sum(src, wt, AIDED, j)
            came = jnp.concatenate([A[:, cols_of(j)], B[:, cols_of(j)]], axis=0)
            sai[:, cols_of(j)] = (acc + came.astype(F32)).astype(BF)

        loop(8, body)
        return send(sai.at[lo], fR.at[lo], left), send(sai.at[hi], fL.at[hi], right)

    v1 = rs_far(actb, wt_off, vA, vB)
    v2 = rs_near(actb, wt_off, vL, vR)
    d3 = w_mid(downb, DSZ, d2)
    rs_own(actb, wt_off)
    sent(*m1, *m2)
    v3 = rs_aided(actb, wt_off, vA, vB, v1, vL, vR)
    d4 = w_end(downb, DSZ, d3)
    arrived((d2[2], d3[2], d3[3], d4))
    p_gh(oh, 0, 4 * T, 0)
    arrived(v2 + v3)

    def weigh(j):
        cols = cols_of(j)
        gap = pown[:, cols] + vL[:, cols].astype(F32) + vR[:, cols].astype(F32)
        rows = rows_in[:, cols]
        res = rows[1:2] * gap + rows[0:1] * adj_in[:, cols].astype(F32)
        modb[0, :, cols] = res.astype(BF)

    loop(8, weigh)
    w1 = xg_start(modb.at[0], modb)

    sent(*v1, *v2, *v3)
    j1 = rs_far(ghb, wt_up, jA, jB)
    j2 = rs_near(ghb, wt_up, jL, jR)
    rs_own(ghb, wt_up)
    w2 = xg_mid(modb, w1)
    j3 = rs_aided(ghb, wt_up, jA, jB, j1, jL, jR)

    sent(*o1, o2a, o2b, *o3, o4a, o4b, o4c, o4d, o5)
    arrived(w2)

    def g_part(zz):
        def body(yy):
            cols = pl.ds(pl.multiple_of((yy * 4 + zz) * 384, 384), 384)
            wt = modb[:, :, cols].reshape(4 * T, 384).T
            for h in range(2):
                ofs[h, yy, zz] = dot(wt, actb[h], NN).astype(BF).reshape(2, 192, HH)

        loop(2, body)
        return send(ofs.at[:, :, zz, 1 - c], gcore.at[:, :, zz], sib)

    def g_add(zz, halves, extra=None):
        def body(yy):
            for h in halves:
                total = ofs[h, yy, zz, c].astype(F32) + gcore[h, yy, zz].astype(F32)
                if extra is not None:
                    total = total + extra[yy].astype(F32)
                ofs[h, yy, zz, c] = total.astype(BF)

        loop(2, body)

    c_op = g_part(z_op)
    c_dn = g_part(z_dn)
    arrived((c_op,))
    g_add(z_op, (0, 1))
    q1 = (
        send(ofs.at[0, :, z_op, c], zA, zleft),
        send(ofs.at[1, :, z_op, c], zB, zright),
    )
    c_up = g_part(z_up)
    arrived((c_dn, c_up))
    g_add(z_dn, (1,))
    q2a = send(ofs.at[1, :, z_dn, c], zR.at[1], zleft)
    g_add(z_up, (0,))
    q2b = send(ofs.at[0, :, z_up, c], zL.at[0], zright)
    c_own = g_part(z)
    arrived(q1)
    g_add(z_dn, (0,), zA)
    q3a = send(ofs.at[0, :, z_dn, c], zR.at[0], zleft)
    g_add(z_up, (1,), zB)
    q3b = send(ofs.at[1, :, z_up, c], zL.at[1], zright)

    arrived(j2 + j3)

    def finish(j):
        cols = cols_of(j)
        gm_out[:, cols] = pown[:, cols] + jL[:, cols].astype(F32) + jR[:, cols].astype(F32)

    loop(8, finish)

    arrived((c_own, q2a, q2b, q3a, q3b))

    def g_sum(yy):
        h, k = yy // 2, yy % 2
        return (
            ofs[h, k, z, c].astype(F32)
            + gcore[h, k, z].astype(F32)
            + zL[h, k].astype(F32)
            + zR[h, k].astype(F32)
        )

    def g_out(i, target):
        yy = (y_op, y_up, y_dn)[i]
        ysum[i] = g_sum(yy).astype(BF)
        return send(ysum.at[i], yr.at[i], target)

    e = [g_out(0, yfar), g_out(1, yright), g_out(2, yleft)]
    og_out[...] = g_sum(y)
    arrived(e)
    og_out[...] = (
        og_out[...] + yr[0].astype(F32) + yr[1].astype(F32) + yr[2].astype(F32)
    ) * (1.0 / 128.0)
    for m in list(unsent.values()):
        sent(m)


def fused(mod, gated, adj, rows, up, down, off):
    hbm = pl.BlockSpec(memory_space=pl.ANY)
    vmem = pl.BlockSpec(memory_space=pltpu.VMEM)
    V = pltpu.VMEM
    flops = 5 * 2 * 1024 * D * HH
    return pl.pallas_call(
        kernel,
        out_shape=(
            jax.ShapeDtypeStruct((T, D), F32),
            jax.ShapeDtypeStruct((192, HH), F32),
        ),
        in_specs=[hbm, hbm, vmem, vmem, hbm, hbm, hbm],
        out_specs=(vmem, vmem),
        scratch_shapes=[
            V((4, T, D), BF), V((4, T, D), BF),
            V((2, D, HH), BF), V((2, HH, D), BF),
            V((2, 2, 4, 2, 192, HH), BF),
            V((2, 4 * T, HH), BF), V((2, 4 * T, HH), F32), V((2, 4 * T, HH), BF),
            V((T, D), BF), V((T, D), BF), V((T, D), BF), V((T, D), F32),
            V((64, D), BF), V((64, D), BF), V((T, D), BF), V((T, D), BF),
            V((64, D), BF), V((64, D), BF), V((T, D), BF), V((T, D), BF),
            V((2, 2, 4, 192, HH), BF),
            V((2, 192, HH), BF), V((2, 192, HH), BF),
            V((2, 2, 192, HH), BF), V((2, 2, 192, HH), BF),
            V((3, 192, HH), BF), V((3, 192, HH), BF),
            pltpu.SemaphoreType.DMA((N_MSG,)),
            pltpu.SemaphoreType.DMA((N_MSG,)),
            pltpu.SemaphoreType.DMA((5,)),
        ],
        compiler_params=pltpu.CompilerParams(
            collective_id=0, has_side_effects=True, vmem_limit_bytes=64 << 20
        ),
        cost_estimate=pl.CostEstimate(flops=flops, bytes_accessed=40 << 20, transcendentals=1 << 20),
        name="fused_step",
    )(mod, gated, adj, rows, up, down, off)


def per_device(states, adjoint, step_index, modulation, up, down, offset):
    step_count = modulation.shape[0]
    index = step_index[0]
    mods = lax.dynamic_index_in_dim(modulation, index, 0, keepdims=False)
    shift, scale, gate = mods[0:1], mods[1:2], mods[2:3]
    timing = (index.astype(F32) + 1.0) / (step_count + 1.0)
    variance = 2.0 * (1.0 - timing) / timing
    inputs = states[0].astype(F32)
    mean = jnp.mean(inputs, axis=-1, keepdims=True)
    var = jnp.mean((inputs - mean) ** 2, axis=-1, keepdims=True)
    rstd = lax.rsqrt(var + 1e-06)
    normed = (inputs - mean) * rstd
    modulated = (normed * (1.0 + scale) + shift).astype(BF)
    adj = adjoint[0]
    gated = (adj.astype(F32) * gate).astype(BF)
    rows = jnp.concatenate([gate, 2.0 / variance * gate * gate] + [gate] * 6, axis=0)
    grad_mod, offset_grad = fused(modulated, gated, adj, rows, up, down, offset)
    scaled = grad_mod * (1.0 + scale)
    adjoint_rate = rstd * (
        scaled
        - jnp.mean(scaled, axis=-1, keepdims=True)
        - normed * jnp.mean(scaled * normed, axis=-1, keepdims=True)
    )
    return adjoint_rate[None], offset_grad


def solution(mesh):
    in_specs = (
        P("dp", "mp", None),
        P("dp", "mp", None),
        P("dp"),
        P(),
        P(None, "mp"),
        P("mp", None),
        P("dp", "mp"),
    )
    out_specs = (P("dp", "mp", None), P("dp", "mp"))
    return jax.shard_map(
        per_device, mesh=mesh, in_specs=in_specs, out_specs=out_specs, check_vma=False
    )
```

```python
import functools
import math

import jax
import jax.numpy as jnp
from jax import lax
from jax.experimental import pallas as pl
from jax.experimental.pallas import tpu as pltpu
from jax.sharding import PartitionSpec as P

MESH = pl.DeviceIdType.MESH
BF = jnp.bfloat16
F32 = jnp.float32
D = 3072
T = 128
HH = 768
NT = (((1,), (1,)), ((), ()))
NN = (((1,), (0,)), ((), ()))
N_MSG = 144


def gelu_both(value):
    coeff = math.sqrt(2.0 / math.pi)
    square = value * value
    tangent = jnp.tanh(coeff * value * (1.0 + 0.044715 * square))
    half = 0.5 * (1.0 + tangent)
    slope = half + 0.5 * value * (1.0 - tangent * tangent) * coeff * (1.0 + 3.0 * 0.044715 * square)
    return value * half, slope


def dot(a, b, dims):
    return lax.dot_general(a, b, dims, preferred_element_type=F32)


def loop(count, body):
    def step(i, carry):
        body(i)
        return carry

    lax.fori_loop(0, count, step, 0)


def kernel(
    st_in, adj_in, rows_in, up_in, down_in, off_in,
    rate_out, og_out,
    modb, gatb, upb, downb, ofs, actb, slp, ghb, sact, swgt, sopp, sun, sai, aid,
    vA, vB, vL, vR, jA, jB, jL, jR, zA, zB, zL, zR, yA, yB, yL, yR, ysum, yr, zsum, zr,
    ss, rs, ls,
):
    dp, mp = lax.axis_index("dp"), lax.axis_index("mp")
    c, z, yl = dp % 2, (dp // 2) % 4, dp // 8
    x, yh = mp % 4, mp // 4
    y = yh * 2 + yl

    def dev(xx, yy, zz, cc):
        return (((yy % 2) * 4 + zz) * 2 + cc, (yy // 2) * 4 + xx)

    right, left = dev((x + 1) % 4, y, z, c), dev((x + 3) % 4, y, z, c)
    z_up, z_dn, z_op = (z + 1) % 4, (z + 3) % 4, (z + 2) % 4
    y_up, y_dn, y_op = (y + 1) % 4, (y + 3) % 4, (y + 2) % 4
    zright, zleft, zfar = dev(x, y, z_up, c), dev(x, y, z_dn, c), dev(x, y, z_op, c)
    yright, yleft, yfar = dev(x, y_up, z, c), dev(x, y_dn, z, c), dev(x, y_op, z, c)
    ypair = dev(x, 3 - y, z, c)
    sib = dev(x, y, z, 1 - c)
    oh = 1 - yh

    count = [0]
    unsent = {}

    def send(src, dst, device):
        i = count[0]
        count[0] += 1
        msg = pltpu.make_async_remote_copy(
            src_ref=src, dst_ref=dst, send_sem=ss.at[i], recv_sem=rs.at[i],
            device_id=device, device_id_type=MESH,
        )
        msg.start()
        unsent[id(msg)] = msg
        return msg

    def sent(msgs):
        for m in msgs:
            m.wait_send()
            del unsent[id(m)]

    def arrived(msgs):
        for m in msgs:
            m.wait_recv()

    def local(i, src, dst):
        copy = pltpu.make_async_copy(src, dst, ls.at[i])
        copy.start()
        return copy

    l_up = local(0, up_in, upb.at[yh])
    l_off = local(1, off_in, ofs.at[yh, c, yl, z])
    l_down = local(2, down_in, downb.at[yh])

    barrier = pltpu.get_barrier_semaphore()
    peers = (right, left, zright, zleft, zfar, yright, yleft, yfar, sib)
    for peer in peers:
        pl.semaphore_signal(barrier, inc=1, device_id=peer, device_id_type=MESH)
    pl.semaphore_wait(barrier, len(peers))

    lo, hi = pl.ds(0, T // 2), pl.ds(T // 2, T // 2)
    E0, E1 = pl.ds(0, 384), pl.ds(384, 384)

    def ring_start(src, own, nxt, prv):
        return [send(src, own, nxt), send(src, own, prv)]

    def ring_mid(first, from_prv, from_nxt, nxt, prv):
        first[0].wait_recv()
        a = send(from_prv, from_prv, nxt)
        first[1].wait_recv()
        b = send(from_nxt, from_nxt, prv)
        return [a, b]

    def xg_start(buf, cols):
        src = buf.at[0, :, cols]
        return [send(src, buf.at[1, :, cols], right), send(src, buf.at[2, :, cols], left)]

    def xg_mid(buf, cols, first):
        first[0].wait_recv()
        a = send(buf.at[1, lo, cols], buf.at[3, lo, cols], right)
        first[1].wait_recv()
        b = send(buf.at[2, hi, cols], buf.at[3, hi, cols], left)
        return [a, b]

    def piece(buf, zz, size, half=None):
        first = (zz * 2 + c) * size
        if half is None:
            return buf.at[oh, pl.ds(first, size)]
        return buf.at[oh, pl.ds(first + half * (size // 2), size // 2)]

    def w_start(src, buf, size):
        r = pl.ds((z * 2 + c) * size, size)
        return send(src.at[r], buf.at[yh, r], ypair)

    def w_ring(buf, size, first):
        first.wait_recv()
        p = piece(buf, z, size)
        return ring_start(p, p, zright, zleft) + [send(p, p, sib)]

    def w_mid(buf, size, msgs):
        out = ring_mid(msgs, piece(buf, z_dn, size, 0), piece(buf, z_up, size, 1), zright, zleft)
        p, q = piece(buf, z_dn, size), piece(buf, z_up, size)
        return out + [send(p, p, sib), send(q, q, sib)]

    def w_end(buf, size, msgs):
        arrived(msgs[:2])
        p = piece(buf, z_op, size)
        return [send(p, p, sib)]

    USZ, DSZ = D // 8, HH // 8
    ALL = pl.ds(0, D)

    def oblock(yy, zz, cols, half=None):
        rows = pl.ds(0, 192) if half is None else pl.ds(96 * half, 96)
        return ofs.at[yy // 2, c, yy % 2, zz, rows, cols]

    def ybundle(yy, half=None):
        zs = pl.ds(0, 4) if half is None else pl.ds(2 * half, 2)
        return ofs.at[yy // 2, c, yy % 2, zs, :, E0]

    def zbundle(zz, half=None):
        hs = pl.ds(0, 2) if half is None else pl.ds(half, 1)
        return ofs.at[hs, c, :, zz, :, E1]

    u1 = w_start(up_in, upb, USZ)
    oA = ring_start(off_in.at[:, E0], oblock(y, z, E0), zright, zleft)
    oB = ring_start(off_in.at[:, E1], oblock(y, z, E1), yright, yleft)

    def norm_of(rows):
        inputs = st_in[rows, :].astype(F32)
        mean = jnp.mean(inputs, axis=-1, keepdims=True)
        cent = inputs - mean
        var = jnp.mean(cent * cent, axis=-1, keepdims=True)
        rstd = lax.rsqrt(var + 1e-06)
        return cent * rstd, rstd

    def prepare(i):
        rows = pl.ds(pl.multiple_of(i * 16, 16), 16)
        normed, _ = norm_of(rows)
        modb[0, rows, :] = (normed * rows_in[3:4, :] + rows_in[2:3, :]).astype(BF)
        gatb[0, rows, :] = (adj_in[rows, :].astype(F32) * rows_in[0:1, :]).astype(BF)

    loop(T // 16, prepare)
    m1 = xg_start(modb, ALL)

    def p_hidden(h, row0, rows, slot0):
        def body(j):
            cols = pl.ds(pl.multiple_of(j * 256, 256), 256)
            mod = modb[pl.ds(slot0, rows // T)].reshape(rows, D)
            act, slope = gelu_both(dot(mod, upb[h, :, cols], NN))
            actb[h, pl.ds(row0, rows), cols] = act.astype(BF)
            slp[h, pl.ds(row0, rows), cols] = slope

        loop(HH // 256, body)

    def p_gh(h, row0, rows, slot0):
        def body(j):
            off = pl.multiple_of(j * 256, 256)
            cols = pl.ds(off, 256)
            gat = gatb[pl.ds(slot0, rows // T)].reshape(rows, D)
            grad = dot(gat, downb[h, pl.ds(off, 256), :], NT)
            ghb[h, pl.ds(row0, rows), cols] = (grad * slp[h, pl.ds(row0, rows), cols]).astype(BF)

        loop(HH // 256, body)

    l_up.wait()
    p_hidden(yh, 0, T, 0)

    l_off.wait()
    oA2 = ring_mid(oA, oblock(y, z_dn, E0, 0), oblock(y, z_up, E0, 1), zright, zleft)
    oB2 = ring_mid(oB, oblock(y_dn, z, E1, 0), oblock(y_up, z, E1, 1), yright, yleft)
    arrived(oA2)
    yb = ybundle(y)
    oC = ring_start(yb, yb, yright, yleft) + [send(yb, yb, sib)]
    arrived(oB2)
    u2 = w_ring(upb, USZ, u1)
    zb = zbundle(z)
    oD = ring_start(zb, zb, zright, zleft) + [send(zb, zb, sib)]

    m2 = xg_mid(modb, ALL, m1)
    g1 = xg_start(gatb, ALL)
    p_hidden(yh, T, 2 * T, 1)
    u3 = w_mid(upb, USZ, u2)
    arrived(m2)
    p_hidden(yh, 3 * T, T, 3)
    a1 = send(actb.at[yh], sact.at[yh], sib)

    oC2 = ring_mid(oC, ybundle(y_dn, 0), ybundle(y_up, 1), yright, yleft)
    d1 = w_start(down_in, downb, DSZ)
    yd, yu = ybundle(y_dn), ybundle(y_up)
    oC3 = [send(yd, yd, sib), send(yu, yu, sib)]
    oD2 = ring_mid(oD, zbundle(z_dn, 0), zbundle(z_up, 1), zright, zleft)
    zd, zu = zbundle(z_dn), zbundle(z_up)
    oD3 = [send(zd, zd, sib), send(zu, zu, sib)]
    u4 = w_end(upb, USZ, u3)

    g2 = xg_mid(gatb, ALL, g1)
    arrived([u2[2], u3[2], u3[3]] + u4)
    p_hidden(oh, 0, 4 * T, 0)
    a2 = send(actb.at[oh], sact.at[oh], sib)
    arrived(oC2)
    yo = ybundle(y_op)
    oC4 = [send(yo, yo, sib)]
    arrived(oD2)
    zo = zbundle(z_op)
    oD4 = [send(zo, zo, sib)]
    d2 = w_ring(downb, DSZ, d1)
    arrived([oC[2], oD[2]] + oC3 + oC4 + oD3 + oD4)

    def sum_chunk(src, wt, q, k):
        cols = pl.ds(q * 768, 768)
        acc = dot(src[0], wt[0], NT) + dot(src[1], wt[1], NT)
        rate_out[:, cols] = acc[0:T]
        sopp[:, cols] = acc[3 * T :].astype(BF)
        sun[:, cols] = acc[T + 64 : 2 * T + 64].astype(BF)
        aid[k, 0:64, :] = acc[T : T + 64]
        aid[k, 64:T, :] = acc[2 * T + 64 : 3 * T]

    def send_far(cols, A, B):
        return [
            send(sopp.at[lo, cols], A.at[:, cols], left),
            send(sopp.at[hi, cols], B.at[:, cols], right),
        ]

    def send_near(cols, fL, fR):
        return [
            send(sun.at[lo, cols], fR.at[hi, cols], left),
            send(sun.at[hi, cols], fL.at[lo, cols], right),
        ]

    def add_aided(q, k, A, B):
        cols = pl.ds(q * 768, 768)
        sai[lo, cols] = (aid[k, 0:64, :] + A[:, cols].astype(F32)).astype(BF)
        sai[hi, cols] = (aid[k, 64:T, :] + B[:, cols].astype(F32)).astype(BF)

    def send_aided(cols, fL, fR):
        return [
            send(sai.at[lo, cols], fR.at[lo, cols], left),
            send(sai.at[hi, cols], fL.at[hi, cols], right),
        ]

    order = ((0, 0), (1, 0), (0, 1), (1, 1))

    def chunk_of(i):
        return order[i][0] * 2 + order[i][1]

    def ccols(i):
        return pl.ds(chunk_of(i) * 768, 768)

    def gap_calc(i):
        cc, ll = order[i]
        wt = [ofs[h, cc, ll].reshape(768, HH) for h in range(2)]
        sum_chunk((actb[0], actb[1]), wt, chunk_of(i), i % 2)
        return send_far(ccols(i), vA, vB), send_near(ccols(i), vL, vR)

    def gap_aided(i, far):
        arrived(far)
        add_aided(chunk_of(i), i % 2, vA, vB)
        return send_aided(ccols(i), vL, vR)

    def pick(value, i):
        cc, ll = order[i]
        parts = [value[:, 384 * k + 192 * cc : 384 * k + 192 * cc + 192] for k in range(4)]
        return jnp.concatenate(parts, axis=1)

    def weigh(i, near, aided):
        arrived(near + aided)
        ll = order[i][1]
        block = pl.ds(1536 * ll, 1536)
        rows = pick(rows_in[:, block], i)

        def body(t):
            r = pl.ds(pl.multiple_of(t * 32, 32), 32)
            adj = pick(adj_in[r, block].astype(F32), i)
            cols = ccols(i)
            gap = rate_out[r, cols] + vL[r, cols].astype(F32) + vR[r, cols].astype(F32)
            modb[0, r, cols] = (rows[1:2] * gap + rows[0:1] * adj).astype(BF)

        loop(T // 32, body)
        return xg_start(modb, ccols(i))

    sent(m1 + m2)
    f0, n0 = gap_calc(0)
    l_down.wait()
    p_gh(yh, 0, T, 0)
    f1, n1 = gap_calc(1)
    b0 = gap_aided(0, f0)
    p_gh(yh, T, 2 * T, 1)
    arrived(g2)
    p_gh(yh, 3 * T, T, 3)
    b1 = gap_aided(1, f1)
    f2, n2 = gap_calc(2)
    w1 = [weigh(0, n0, b0)]
    f3, n3 = gap_calc(3)
    b2 = gap_aided(2, f2)
    w1.append(weigh(1, n1, b1))
    d3 = w_mid(downb, DSZ, d2)
    b3 = gap_aided(3, f3)
    w2 = [xg_mid(modb, ccols(0), w1[0])]
    w1.append(weigh(2, n2, b2))
    w2.append(xg_mid(modb, ccols(1), w1[1]))
    w1.append(weigh(3, n3, b3))
    d4 = w_end(downb, DSZ, d3)
    arrived([d2[2], d3[2], d3[3]] + d4)
    p_gh(oh, 0, 4 * T, 0)
    w2.append(xg_mid(modb, ccols(2), w1[2]))
    sent(f0 + f1 + f2 + f3 + n0 + n1 + n2 + n3 + b0 + b1 + b2 + b3)

    def adj_calc(q):
        wt = [upb[h, q * 768 : q * 768 + 768, :] for h in range(2)]
        sum_chunk((ghb[0], ghb[1]), wt, q, q)

    def swg(ll, half):
        mine = half * 1536 + ll * 768
        return pl.ds(pl.multiple_of(mine, 768), 768)

    def to_sib(ll):
        cols = swg(ll, 1 - c)
        return send(modb.at[:, :, cols], swgt.at[ll], sib)

    adj_calc(0)
    adj_calc(1)
    w2.append(xg_mid(modb, ccols(3), w1[3]))
    arrived(w2[0] + w2[1])
    s0 = to_sib(0)
    adj_calc(2)
    adj_calc(3)
    jf = [send_far(pl.ds(0, 1536), jA, jB), send_far(pl.ds(1536, 1536), jA, jB)]
    jn = [send_near(pl.ds(0, 1536), jL, jR), send_near(pl.ds(1536, 1536), jL, jR)]
    arrived(w2[2] + w2[3])
    s1 = to_sib(1)

    sent(oA + oA2 + oB + oB2 + oC + oC2 + oC3 + oC4 + oD + oD2 + oD3 + oD4)
    arrived([a1, a2, s0, s1])

    def g_tile(h, ll, zp):
        mine = pl.multiple_of(c * 1536 + ll * 768 + zp * 384, 384)
        theirs = pl.multiple_of(zp * 384, 384)
        own = modb[:, :, pl.ds(mine, 384)].reshape(4 * T, 384).T
        other = swgt[ll, :, :, pl.ds(theirs, 384)].reshape(4 * T, 384).T
        acc = dot(own, actb[h], NN) + dot(other, sact[h], NN)
        ofs[h, c, ll, pl.ds(2 * zp, 2)] = acc.astype(BF).reshape(2, 192, HH)

    zpA, zpB = z_op // 2, z // 2

    def gy(yy, zs):
        return ofs.at[yy // 2, c, yy % 2, zs, :, E1]

    def gz(h, zz):
        return ofs.at[h, c, :, zz, :, E0]

    Z01, Z23 = pl.ds(0, 2), pl.ds(2, 2)
    g_tile(oh, yl, zpA)
    g_tile(oh, yl, zpB)
    ey1 = [send(gy(y_op, Z01), yA, yleft), send(gy(y_op, Z23), yB, yright)]
    g_tile(oh, 1 - yl, zpA)
    g_tile(yh, yl, zpA)
    g_tile(yh, 1 - yl, zpA)
    ez1 = [send(gz(0, z_op), zA, zleft), send(gz(1, z_op), zB, zright)]
    g_tile(oh, 1 - yl, zpB)
    g_tile(yh, 1 - yl, zpB)
    ey2 = [send(gy(y_dn, Z23), yR.at[Z23], yleft), send(gy(y_up, Z01), yL.at[Z01], yright)]
    g_tile(yh, yl, zpB)
    ez2 = [send(gz(1, z_dn), zR.at[1], zleft), send(gz(0, z_up), zL.at[0], zright)]

    def add_y(yy, z0, extra):
        def body(k):
            ref = ofs.at[yy // 2, c, yy % 2, z0 + k, :, E1]
            ref[...] = (ref[...].astype(F32) + extra[k].astype(F32)).astype(BF)

        loop(2, body)

    def add_z(h, zz, extra):
        def body(k):
            ref = ofs.at[h, c, k, zz, :, E0]
            ref[...] = (ref[...].astype(F32) + extra[k].astype(F32)).astype(BF)

        loop(2, body)

    arrived(ey1)
    add_y(y_dn, 0, yA)
    ey3 = [send(gy(y_dn, Z01), yR.at[Z01], yleft)]
    add_y(y_up, 2, yB)
    ey3.append(send(gy(y_up, Z23), yL.at[Z23], yright))
    arrived(ez1)
    add_z(0, z_dn, zA)
    ez3 = [send(gz(0, z_dn), zR.at[0], zleft)]
    add_z(1, z_up, zB)
    ez3.append(send(gz(1, z_up), zL.at[1], zright))

    jb = []
    for half in range(2):
        arrived(jf[half])
        for q in (2 * half, 2 * half + 1):
            add_aided(q, q, jA, jB)
        jb.append(send_aided(pl.ds(1536 * half, 1536), jL, jR))

    arrived(ey2 + ey3)

    def y_total(zz):
        return ofs[yh, c, yl, zz, :, E1].astype(F32) + yL[zz].astype(F32) + yR[zz].astype(F32)

    ez4 = []
    for k, (zz, target) in enumerate(((z_op, zfar), (z_up, zright), (z_dn, zleft))):
        zsum[k] = y_total(zz).astype(BF)
        ez4.append(send(zsum.at[k], zr.at[k], target))
    arrived(ez2 + ez3)

    def z_total(yy):
        h, k = yy // 2, yy % 2
        return ofs[h, c, k, z, :, E0].astype(F32) + zL[h, k].astype(F32) + zR[h, k].astype(F32)

    ey4 = []
    for k, (yy, target) in enumerate(((y_op, yfar), (y_up, yright), (y_dn, yleft))):
        ysum[k] = z_total(yy).astype(BF)
        ey4.append(send(ysum.at[k], yr.at[k], target))

    for half in range(2):
        arrived(jn[half] + jb[half])

    def finish(i):
        rows = pl.ds(pl.multiple_of(i * 16, 16), 16)
        normed, rstd = norm_of(rows)
        total = rate_out[rows, :] + jL[rows, :].astype(F32) + jR[rows, :].astype(F32)
        scaled = total * rows_in[3:4, :]
        mean = jnp.mean(scaled, axis=-1, keepdims=True)
        cross = jnp.mean(scaled * normed, axis=-1, keepdims=True)
        rate_out[rows, :] = rstd * (scaled - mean - normed * cross)

    loop(T // 16, finish)

    og_out[:, E1] = y_total(z)
    og_out[:, E0] = z_total(y)
    arrived(ez4)
    og_out[:, E1] = (
        og_out[:, E1] + zr[0].astype(F32) + zr[1].astype(F32) + zr[2].astype(F32)
    ) * (1.0 / 128.0)
    arrived(ey4)
    og_out[:, E0] = (
        og_out[:, E0] + yr[0].astype(F32) + yr[1].astype(F32) + yr[2].astype(F32)
    ) * (1.0 / 128.0)
    for m in list(unsent.values()):
        m.wait_send()


def fused(states, adj, rows, up, down, off):
    hbm = pl.BlockSpec(memory_space=pl.ANY)
    vmem = pl.BlockSpec(memory_space=pltpu.VMEM)
    V = pltpu.VMEM
    flops = 5 * 2 * 1024 * D * HH
    return pl.pallas_call(
        kernel,
        out_shape=(
            jax.ShapeDtypeStruct((T, D), F32),
            jax.ShapeDtypeStruct((192, HH), F32),
        ),
        in_specs=[vmem, vmem, vmem, hbm, hbm, hbm],
        out_specs=(vmem, vmem),
        scratch_shapes=[
            V((4, T, D), BF), V((4, T, D), BF),
            V((2, D, HH), BF), V((2, HH, D), BF),
            V((2, 2, 2, 4, 192, HH), BF),
            V((2, 4 * T, HH), BF), V((2, 4 * T, HH), F32), V((2, 4 * T, HH), BF),
            V((2, 4 * T, HH), BF), V((2, 4, T, HH), BF),
            V((T, D), BF), V((T, D), BF), V((T, D), BF),
            V((4, T, HH), F32),
            V((64, D), BF), V((64, D), BF), V((T, D), BF), V((T, D), BF),
            V((64, D), BF), V((64, D), BF), V((T, D), BF), V((T, D), BF),
            V((2, 192, 384), BF), V((2, 192, 384), BF),
            V((2, 2, 192, 384), BF), V((2, 2, 192, 384), BF),
            V((2, 192, 384), BF), V((2, 192, 384), BF),
            V((4, 192, 384), BF), V((4, 192, 384), BF),
            V((3, 192, 384), BF), V((3, 192, 384), BF),
            V((3, 192, 384), BF), V((3, 192, 384), BF),
            pltpu.SemaphoreType.DMA((N_MSG,)),
            pltpu.SemaphoreType.DMA((N_MSG,)),
            pltpu.SemaphoreType.DMA((3,)),
        ],
        compiler_params=pltpu.CompilerParams(
            collective_id=0, has_side_effects=True, vmem_limit_bytes=64 << 20
        ),
        cost_estimate=pl.CostEstimate(flops=flops, bytes_accessed=40 << 20, transcendentals=1 << 20),
        name="fused_step",
    )(states, adj, rows, up, down, off)


def per_device(states, adjoint, step_index, modulation, up, down, offset):
    step_count = modulation.shape[0]
    index = step_index[0]
    mods = lax.dynamic_index_in_dim(modulation, index, 0, keepdims=False)
    shift, scale, gate = mods[0:1], mods[1:2], mods[2:3]
    timing = (index.astype(F32) + 1.0) / (step_count + 1.0)
    variance = 2.0 * (1.0 - timing) / timing
    rows = jnp.concatenate(
        [gate, 2.0 / variance * gate * gate, shift, 1.0 + scale] + [gate] * 4, axis=0
    )
    rate, offset_grad = fused(states[0], adjoint[0], rows, up, down, offset)
    return rate[None], offset_grad


def solution(mesh):
    in_specs = (
        P("dp", "mp", None),
        P("dp", "mp", None),
        P("dp"),
        P(),
        P(None, "mp"),
        P("mp", None),
        P("dp", "mp"),
    )
    out_specs = (P("dp", "mp", None), P("dp", "mp"))
    return jax.shard_map(
        per_device, mesh=mesh, in_specs=in_specs, out_specs=out_specs, check_vma=False
    )
```

```python
import functools
import math

import jax
import jax.numpy as jnp
from jax import lax
from jax.experimental import pallas as pl
from jax.experimental.pallas import tpu as pltpu
from jax.sharding import PartitionSpec as P

MESH = pl.DeviceIdType.MESH
BF = jnp.bfloat16
F32 = jnp.float32
D = 3072
T = 128
HH = 768
NT = (((1,), (1,)), ((), ()))
NN = (((1,), (0,)), ((), ()))
N_MSG = 160


def gelu_both(value):
    coeff = math.sqrt(2.0 / math.pi)
    square = value * value
    tangent = jnp.tanh(coeff * value * (1.0 + 0.044715 * square))
    half = 0.5 * (1.0 + tangent)
    slope = half + 0.5 * value * (1.0 - tangent * tangent) * coeff * (1.0 + 3.0 * 0.044715 * square)
    return value * half, slope


def dot(a, b, dims):
    return lax.dot_general(a, b, dims, preferred_element_type=F32)


def loop(count, body):
    def step(i, carry):
        body(i)
        return carry

    lax.fori_loop(0, count, step, 0)


def kernel(
    st_hbm, adj_hbm, rows_hbm, up_in, down_in, off_in,
    rate_out, og_out,
    st_in, adj_in, rows_in, modb, gatb, upb, downb, ofs, actb, slp, ghb, sact, swgt, sopp, sun, sai, aid,
    vA, vB, vL, vR, jA, jB, jL, jR, zA, zB, zL, zR, yA, yB, yL, yR, ysum, yr, zsum, zr,
    ss, rs, ls,
):
    dp, mp = lax.axis_index("dp"), lax.axis_index("mp")
    c, z, yl = dp % 2, (dp // 2) % 4, dp // 8
    x, yh = mp % 4, mp // 4
    y = yh * 2 + yl

    def dev(xx, yy, zz, cc):
        return (((yy % 2) * 4 + zz) * 2 + cc, (yy // 2) * 4 + xx)

    right, left = dev((x + 1) % 4, y, z, c), dev((x + 3) % 4, y, z, c)
    z_up, z_dn, z_op = (z + 1) % 4, (z + 3) % 4, (z + 2) % 4
    y_up, y_dn, y_op = (y + 1) % 4, (y + 3) % 4, (y + 2) % 4
    zright, zleft, zfar = dev(x, y, z_up, c), dev(x, y, z_dn, c), dev(x, y, z_op, c)
    yright, yleft, yfar = dev(x, y_up, z, c), dev(x, y_dn, z, c), dev(x, y_op, z, c)
    ypair = dev(x, 3 - y, z, c)
    sib = dev(x, y, z, 1 - c)
    oh = 1 - yh

    count = [0]
    unsent = {}

    def send(src, dst, device):
        i = count[0]
        count[0] += 1
        msg = pltpu.make_async_remote_copy(
            src_ref=src, dst_ref=dst, send_sem=ss.at[i], recv_sem=rs.at[i],
            device_id=device, device_id_type=MESH,
        )
        msg.start()
        unsent[id(msg)] = msg
        return msg

    def sent(msgs):
        for m in msgs:
            m.wait_send()
            del unsent[id(m)]

    def arrived(msgs):
        for m in msgs:
            m.wait_recv()

    def local(i, src, dst):
        copy = pltpu.make_async_copy(src, dst, ls.at[i])
        copy.start()
        return copy

    barrier = pltpu.get_barrier_semaphore()
    peers = (right, left, zright, zleft, zfar, yright, yleft, yfar, sib)
    for peer in peers:
        pl.semaphore_signal(barrier, inc=1, device_id=peer, device_id_type=MESH)
    l_pre = [local(0, st_hbm, st_in), local(1, adj_hbm, adj_in), local(2, rows_hbm, rows_in)]
    l_up = local(3, up_in, upb.at[yh])
    l_off = local(4, off_in, ofs.at[yh, c, yl, z])
    l_down = local(5, down_in, downb.at[yh])
    pl.semaphore_wait(barrier, len(peers))

    lo, hi = pl.ds(0, T // 2), pl.ds(T // 2, T // 2)
    E0, E1 = pl.ds(0, 512), pl.ds(512, 256)
    G0, G1 = pl.ds(0, 384), pl.ds(384, 384)

    def ring_start(src, own, nxt, prv):
        return [send(src, own, nxt), send(src, own, prv)]

    def ring_mid(first, from_prv, from_nxt, nxt, prv):
        first[0].wait_recv()
        a = send(from_prv, from_prv, nxt)
        first[1].wait_recv()
        b = send(from_nxt, from_nxt, prv)
        return [a, b]

    def xg_start(buf, cols):
        src = buf.at[0, :, cols]
        return [send(src, buf.at[1, :, cols], right), send(src, buf.at[2, :, cols], left)]

    def xg_mid(buf, cols, first):
        first[0].wait_recv()
        a = send(buf.at[1, lo, cols], buf.at[3, lo, cols], right)
        first[1].wait_recv()
        b = send(buf.at[2, hi, cols], buf.at[3, hi, cols], left)
        return [a, b]

    def tok_start(buf):
        def one(rows, slot, device):
            return send(buf.at[0, rows], buf.at[slot, rows], device)

        return [one(lo, 1, right), one(hi, 2, left), one(hi, 1, right), one(lo, 2, left)]

    def tok_mid(buf, first):
        first[0].wait_recv()
        a = send(buf.at[1, lo], buf.at[3, lo], right)
        first[1].wait_recv()
        b = send(buf.at[2, hi], buf.at[3, hi], left)
        return [a, b]

    def piece(buf, zz, part, half=None):
        size, k, n = part
        first, rows = (zz * 2 + c) * size + k * (size // n), size // n
        if half is None:
            return buf.at[oh, pl.ds(first, rows)]
        return buf.at[oh, pl.ds(first + half * (rows // 2), rows // 2)]

    def w_start(src, buf, part):
        size, k, n = part
        r = pl.ds((z * 2 + c) * size + k * (size // n), size // n)
        return send(src.at[r], buf.at[yh, r], ypair)

    def w_ring(buf, part, first):
        first.wait_recv()
        p = piece(buf, z, part)
        return ring_start(p, p, zright, zleft) + [send(p, p, sib)]

    def w_mid(buf, part, msgs):
        out = ring_mid(msgs, piece(buf, z_dn, part, 0), piece(buf, z_up, part, 1), zright, zleft)
        p, q = piece(buf, z_dn, part), piece(buf, z_up, part)
        return out + [send(p, p, sib), send(q, q, sib)]

    def w_end(buf, part, msgs):
        arrived(msgs[:2])
        p = piece(buf, z_op, part)
        return [send(p, p, sib)]

    UA, UB, DP = (D // 8, 0, 2), (D // 8, 1, 2), (HH // 8, 0, 1)

    def oblock(yy, zz, cols, half=None):
        rows = pl.ds(0, 192) if half is None else pl.ds(96 * half, 96)
        return ofs.at[yy // 2, c, yy % 2, zz, rows, cols]

    def ybundle(yy, half=None):
        zs = pl.ds(0, 4) if half is None else pl.ds(2 * half, 2)
        return ofs.at[yy // 2, c, yy % 2, zs, :, E0]

    def zbundle(zz, half=None):
        hs = pl.ds(0, 2) if half is None else pl.ds(half, 1)
        return ofs.at[hs, c, :, zz, :, E1]

    u1a = w_start(up_in, upb, UA)
    oB = ring_start(off_in.at[:, E1], oblock(y, z, E1), yright, yleft)
    oA = ring_start(off_in.at[:, E0], oblock(y, z, E0), zright, zleft)

    def norm_of(rows):
        inputs = st_in[rows, :].astype(F32)
        mean = jnp.mean(inputs, axis=-1, keepdims=True)
        cent = inputs - mean
        var = jnp.mean(cent * cent, axis=-1, keepdims=True)
        rstd = lax.rsqrt(var + 1e-06)
        return cent * rstd, rstd

    def prepare(i):
        rows = pl.ds(pl.multiple_of(i * 16, 16), 16)
        normed, _ = norm_of(rows)
        modb[0, rows, :] = (normed * rows_in[3:4, :] + rows_in[2:3, :]).astype(BF)
        gatb[0, rows, :] = (adj_in[rows, :].astype(F32) * rows_in[0:1, :]).astype(BF)

    for copy in l_pre:
        copy.wait()
    loop(T // 16, prepare)
    m1 = tok_start(modb)

    def p_hidden(h, row0, rows, slot0):
        def body(j):
            cols = pl.ds(pl.multiple_of(j * 256, 256), 256)
            mod = modb[pl.ds(slot0, rows // T)].reshape(rows, D)
            act, slope = gelu_both(dot(mod, upb[h, :, cols], NN))
            actb[h, pl.ds(row0, rows), cols] = act.astype(BF)
            slp[h, pl.ds(row0, rows), cols] = slope

        loop(HH // 256, body)

    def p_gh(h, row0, rows, slot0):
        def body(j):
            off = pl.multiple_of(j * 256, 256)
            cols = pl.ds(off, 256)
            gat = gatb[pl.ds(slot0, rows // T)].reshape(rows, D)
            grad = dot(gat, downb[h, pl.ds(off, 256), :], NT)
            ghb[h, pl.ds(row0, rows), cols] = (grad * slp[h, pl.ds(row0, rows), cols]).astype(BF)

        loop(HH // 256, body)

    l_off.wait()
    oB2 = ring_mid(oB, oblock(y_dn, z, E1, 0), oblock(y_up, z, E1, 1), yright, yleft)
    u1b = w_start(up_in, upb, UB)
    oA2 = ring_mid(oA, oblock(y, z_dn, E0, 0), oblock(y, z_up, E0, 1), zright, zleft)
    u2a = w_ring(upb, UA, u1a)
    arrived(oB2)
    zb = zbundle(z)
    oD = ring_start(zb, zb, zright, zleft) + [send(zb, zb, sib)]
    arrived(oA2)
    yb = ybundle(y)
    oC = ring_start(yb, yb, yright, yleft) + [send(yb, yb, sib)]
    l_up.wait()
    p_hidden(yh, 0, T, 0)
    m2 = tok_mid(modb, m1)
    u3a = w_mid(upb, UA, u2a)
    oD2 = ring_mid(oD, zbundle(z_dn, 0), zbundle(z_up, 1), zright, zleft)
    zd, zu = zbundle(z_dn), zbundle(z_up)
    oD3 = [send(zd, zd, sib), send(zu, zu, sib)]
    u2b = w_ring(upb, UB, u1b)
    arrived(m1[2:])
    g1 = tok_start(gatb)
    p_hidden(yh, T, 2 * T, 1)
    oC2 = ring_mid(oC, ybundle(y_dn, 0), ybundle(y_up, 1), yright, yleft)
    yd, yu = ybundle(y_dn), ybundle(y_up)
    oC3 = [send(yd, yd, sib), send(yu, yu, sib)]
    d1 = w_start(down_in, downb, DP)
    u4a = w_end(upb, UA, u3a)
    u3b = w_mid(upb, UB, u2b)
    arrived(m2)
    p_hidden(yh, 3 * T, T, 3)
    a1 = send(actb.at[yh], sact.at[yh], sib)
    arrived(oD2)
    zo = zbundle(z_op)
    oD4 = [send(zo, zo, sib)]
    u4b = w_end(upb, UB, u3b)
    arrived(oC2)
    yo = ybundle(y_op)
    oC4 = [send(yo, yo, sib)]
    g2 = tok_mid(gatb, g1)
    arrived([u2a[2], u3a[2], u3a[3], u2b[2], u3b[2], u3b[3]] + u4a + u4b)
    p_hidden(oh, 0, 4 * T, 0)
    a2 = send(actb.at[oh], sact.at[oh], sib)
    arrived([oC[2], oD[2]] + oC3 + oC4 + oD3 + oD4)

    def sum_chunk(src, wt, q, k):
        cols = pl.ds(q * 768, 768)
        acc = dot(src[0], wt[0], NT) + dot(src[1], wt[1], NT)
        rate_out[:, cols] = acc[0:T]
        sopp[:, cols] = acc[3 * T :].astype(BF)
        sun[:, cols] = acc[T + 64 : 2 * T + 64].astype(BF)
        aid[k, 0:64, :] = acc[T : T + 64]
        aid[k, 64:T, :] = acc[2 * T + 64 : 3 * T]

    def send_far(cols, A, B):
        return [
            send(sopp.at[lo, cols], A.at[:, cols], left),
            send(sopp.at[hi, cols], B.at[:, cols], right),
        ]

    def send_near(cols, fL, fR):
        return [
            send(sun.at[lo, cols], fR.at[hi, cols], left),
            send(sun.at[hi, cols], fL.at[lo, cols], right),
        ]

    def add_aided(q, k, A, B):
        cols = pl.ds(q * 768, 768)
        sai[lo, cols] = (aid[k, 0:64, :] + A[:, cols].astype(F32)).astype(BF)
        sai[hi, cols] = (aid[k, 64:T, :] + B[:, cols].astype(F32)).astype(BF)

    def send_aided(cols, fL, fR):
        return [
            send(sai.at[lo, cols], fR.at[lo, cols], left),
            send(sai.at[hi, cols], fL.at[hi, cols], right),
        ]

    order = ((0, 0), (1, 0), (0, 1), (1, 1))

    def chunk_of(i):
        return order[i][0] * 2 + order[i][1]

    def ccols(i):
        return pl.ds(chunk_of(i) * 768, 768)

    def gap_calc(i):
        cc, ll = order[i]
        wt = [ofs[h, cc, ll].reshape(768, HH) for h in range(2)]
        sum_chunk((actb[0], actb[1]), wt, chunk_of(i), i % 2)
        return send_far(ccols(i), vA, vB), send_near(ccols(i), vL, vR)

    def gap_aided(i, far):
        arrived(far)
        add_aided(chunk_of(i), i % 2, vA, vB)
        return send_aided(ccols(i), vL, vR)

    def pick(value, i):
        cc, ll = order[i]
        parts = [value[:, 384 * k + 192 * cc : 384 * k + 192 * cc + 192] for k in range(4)]
        return jnp.concatenate(parts, axis=1)

    def weigh(i, near, aided):
        arrived(near + aided)
        ll = order[i][1]
        block = pl.ds(1536 * ll, 1536)
        rows = pick(rows_in[:, block], i)

        def body(t):
            r = pl.ds(pl.multiple_of(t * 32, 32), 32)
            adj = pick(adj_in[r, block].astype(F32), i)
            cols = ccols(i)
            gap = rate_out[r, cols] + vL[r, cols].astype(F32) + vR[r, cols].astype(F32)
            modb[0, r, cols] = (rows[1:2] * gap + rows[0:1] * adj).astype(BF)

        loop(T // 32, body)
        return xg_start(modb, ccols(i))

    sent(m1 + m2)
    f0, n0 = gap_calc(0)
    f1, n1 = gap_calc(1)
    b0 = gap_aided(0, f0)
    f2, n2 = gap_calc(2)
    b1 = gap_aided(1, f1)
    w1 = [weigh(0, n0, b0)]
    d2 = w_ring(downb, DP, d1)
    f3, n3 = gap_calc(3)
    b2 = gap_aided(2, f2)
    w1.append(weigh(1, n1, b1))
    l_down.wait()
    arrived(g1[2:] + g2)
    p_gh(yh, 0, 4 * T, 0)
    b3 = gap_aided(3, f3)
    w2 = [xg_mid(modb, ccols(0), w1[0])]
    w1.append(weigh(2, n2, b2))
    d3 = w_mid(downb, DP, d2)
    w2.append(xg_mid(modb, ccols(1), w1[1]))
    w1.append(weigh(3, n3, b3))
    d4 = w_end(downb, DP, d3)
    sent(f0 + f1 + f2 + f3 + n0 + n1 + n2 + n3 + b0 + b1 + b2 + b3)
    arrived([d2[2], d3[2], d3[3]] + d4)
    p_gh(oh, 0, 4 * T, 0)
    w2.append(xg_mid(modb, ccols(2), w1[2]))

    def adj_calc(q):
        wt = [upb[h, q * 768 : q * 768 + 768, :] for h in range(2)]
        sum_chunk((ghb[0], ghb[1]), wt, q, q)

    def swg(ll, half):
        mine = half * 1536 + ll * 768
        return pl.ds(pl.multiple_of(mine, 768), 768)

    def to_sib(ll):
        cols = swg(ll, 1 - c)
        return send(modb.at[:, :, cols], swgt.at[ll], sib)

    adj_calc(0)
    adj_calc(1)
    w2.append(xg_mid(modb, ccols(3), w1[3]))
    arrived(w2[0] + w2[1])
    s0 = to_sib(0)
    jf = [send_far(pl.ds(0, 1536), jA, jB)]
    jn = [send_near(pl.ds(0, 1536), jL, jR)]
    adj_calc(2)
    arrived(w2[2] + w2[3])
    s1 = to_sib(1)
    adj_calc(3)
    jf.append(send_far(pl.ds(1536, 1536), jA, jB))
    jn.append(send_near(pl.ds(1536, 1536), jL, jR))

    sent(oA + oA2 + oB + oB2 + oC + oC2 + oC3 + oC4 + oD + oD2 + oD3 + oD4)
    arrived([a1, a2, s0, s1])

    def g_tile(h, ll, zp):
        mine = pl.multiple_of(c * 1536 + ll * 768 + zp * 384, 384)
        theirs = pl.multiple_of(zp * 384, 384)
        own = modb[:, :, pl.ds(mine, 384)].reshape(4 * T, 384).T
        other = swgt[ll, :, :, pl.ds(theirs, 384)].reshape(4 * T, 384).T
        acc = dot(own, actb[h], NN) + dot(other, sact[h], NN)
        ofs[h, c, ll, pl.ds(2 * zp, 2)] = acc.astype(BF).reshape(2, 192, HH)

    zpA, zpB = z_op // 2, z // 2

    def gy(yy, zs):
        return ofs.at[yy // 2, c, yy % 2, zs, :, G1]

    def gz(h, zz):
        return ofs.at[h, c, :, zz, :, G0]

    Z01, Z23 = pl.ds(0, 2), pl.ds(2, 2)
    g_tile(oh, yl, zpA)
    g_tile(oh, yl, zpB)
    ey1 = [send(gy(y_op, Z01), yA, yleft), send(gy(y_op, Z23), yB, yright)]
    g_tile(oh, 1 - yl, zpA)
    g_tile(yh, yl, zpA)
    g_tile(yh, 1 - yl, zpA)
    ez1 = [send(gz(0, z_op), zA, zleft), send(gz(1, z_op), zB, zright)]
    g_tile(oh, 1 - yl, zpB)
    g_tile(yh, 1 - yl, zpB)
    ey2 = [send(gy(y_dn, Z23), yR.at[Z23], yleft), send(gy(y_up, Z01), yL.at[Z01], yright)]
    g_tile(yh, yl, zpB)
    ez2 = [send(gz(1, z_dn), zR.at[1], zleft), send(gz(0, z_up), zL.at[0], zright)]

    def add_y(yy, z0, extra):
        def body(k):
            ref = ofs.at[yy // 2, c, yy % 2, z0 + k, :, G1]
            ref[...] = (ref[...].astype(F32) + extra[k].astype(F32)).astype(BF)

        loop(2, body)

    def add_z(h, zz, extra):
        def body(k):
            ref = ofs.at[h, c, k, zz, :, G0]
            ref[...] = (ref[...].astype(F32) + extra[k].astype(F32)).astype(BF)

        loop(2, body)

    arrived(ey1)
    add_y(y_dn, 0, yA)
    ey3 = [send(gy(y_dn, Z01), yR.at[Z01], yleft)]
    add_y(y_up, 2, yB)
    ey3.append(send(gy(y_up, Z23), yL.at[Z23], yright))
    arrived(ez1)
    add_z(0, z_dn, zA)
    ez3 = [send(gz(0, z_dn), zR.at[0], zleft)]
    add_z(1, z_up, zB)
    ez3.append(send(gz(1, z_up), zL.at[1], zright))

    jb = []
    for half in range(2):
        arrived(jf[half])
        for q in (2 * half, 2 * half + 1):
            add_aided(q, q, jA, jB)
        jb.append(send_aided(pl.ds(1536 * half, 1536), jL, jR))

    arrived(ey2 + ey3)

    def y_total(zz):
        return ofs[yh, c, yl, zz, :, G1].astype(F32) + yL[zz].astype(F32) + yR[zz].astype(F32)

    ez4 = []
    for k, (zz, target) in enumerate(((z_op, zfar), (z_up, zright), (z_dn, zleft))):
        zsum[k] = y_total(zz).astype(BF)
        ez4.append(send(zsum.at[k], zr.at[k], target))
    arrived(ez2 + ez3)

    def z_total(yy):
        h, k = yy // 2, yy % 2
        return ofs[h, c, k, z, :, G0].astype(F32) + zL[h, k].astype(F32) + zR[h, k].astype(F32)

    ey4 = []
    for k, (yy, target) in enumerate(((y_op, yfar), (y_up, yright), (y_dn, yleft))):
        ysum[k] = z_total(yy).astype(BF)
        ey4.append(send(ysum.at[k], yr.at[k], target))

    for half in range(2):
        arrived(jn[half] + jb[half])

    def finish(i):
        rows = pl.ds(pl.multiple_of(i * 16, 16), 16)
        normed, rstd = norm_of(rows)
        total = rate_out[rows, :] + jL[rows, :].astype(F32) + jR[rows, :].astype(F32)
        scaled = total * rows_in[3:4, :]
        mean = jnp.mean(scaled, axis=-1, keepdims=True)
        cross = jnp.mean(scaled * normed, axis=-1, keepdims=True)
        rate_out[rows, :] = rstd * (scaled - mean - normed * cross)

    loop(T // 16, finish)

    og_out[:, G1] = y_total(z)
    og_out[:, G0] = z_total(y)
    arrived(ez4)
    og_out[:, G1] = (
        og_out[:, G1] + zr[0].astype(F32) + zr[1].astype(F32) + zr[2].astype(F32)
    ) * (1.0 / 128.0)
    arrived(ey4)
    og_out[:, G0] = (
        og_out[:, G0] + yr[0].astype(F32) + yr[1].astype(F32) + yr[2].astype(F32)
    ) * (1.0 / 128.0)
    for m in list(unsent.values()):
        m.wait_send()


def fused(states, adj, rows, up, down, off):
    hbm = pl.BlockSpec(memory_space=pl.ANY)
    vmem = pl.BlockSpec(memory_space=pltpu.VMEM)
    V = pltpu.VMEM
    flops = 5 * 2 * 1024 * D * HH
    return pl.pallas_call(
        kernel,
        out_shape=(
            jax.ShapeDtypeStruct((T, D), F32),
            jax.ShapeDtypeStruct((192, HH), F32),
        ),
        in_specs=[hbm] * 6,
        out_specs=(vmem, vmem),
        scratch_shapes=[
            V((T, D), BF), V((T, D), BF), V((8, D), F32),
            V((4, T, D), BF), V((4, T, D), BF),
            V((2, D, HH), BF), V((2, HH, D), BF),
            V((2, 2, 2, 4, 192, HH), BF),
            V((2, 4 * T, HH), BF), V((2, 4 * T, HH), F32), V((2, 4 * T, HH), BF),
            V((2, 4 * T, HH), BF), V((2, 4, T, HH), BF),
            V((T, D), BF), V((T, D), BF), V((T, D), BF),
            V((4, T, HH), F32),
            V((64, D), BF), V((64, D), BF), V((T, D), BF), V((T, D), BF),
            V((64, D), BF), V((64, D), BF), V((T, D), BF), V((T, D), BF),
            V((2, 192, 384), BF), V((2, 192, 384), BF),
            V((2, 2, 192, 384), BF), V((2, 2, 192, 384), BF),
            V((2, 192, 384), BF), V((2, 192, 384), BF),
            V((4, 192, 384), BF), V((4, 192, 384), BF),
            V((3, 192, 384), BF), V((3, 192, 384), BF),
            V((3, 192, 384), BF), V((3, 192, 384), BF),
            pltpu.SemaphoreType.DMA((N_MSG,)),
            pltpu.SemaphoreType.DMA((N_MSG,)),
            pltpu.SemaphoreType.DMA((6,)),
        ],
        compiler_params=pltpu.CompilerParams(
            collective_id=0, has_side_effects=True, vmem_limit_bytes=64 << 20
        ),
        cost_estimate=pl.CostEstimate(flops=flops, bytes_accessed=40 << 20, transcendentals=1 << 20),
        name="fused_step",
    )(states, adj, rows, up, down, off)


def per_device(states, adjoint, step_index, modulation, up, down, offset):
    step_count = modulation.shape[0]
    index = step_index[0]
    mods = lax.dynamic_index_in_dim(modulation, index, 0, keepdims=False)
    shift, scale, gate = mods[0:1], mods[1:2], mods[2:3]
    timing = (index.astype(F32) + 1.0) / (step_count + 1.0)
    variance = 2.0 * (1.0 - timing) / timing
    which = lax.broadcasted_iota(jnp.int32, (8, D), 0)
    rows = jnp.where(
        which == 0,
        gate,
        jnp.where(which == 1, 2.0 / variance * gate * gate, jnp.where(which == 2, shift, 1.0 + scale)),
    )
    rate, offset_grad = fused(states[0], adjoint[0], rows, up, down, offset)
    return rate[None], offset_grad


def solution(mesh):
    in_specs = (
        P("dp", "mp", None),
        P("dp", "mp", None),
        P("dp"),
        P(),
        P(None, "mp"),
        P("mp", None),
        P("dp", "mp"),
    )
    out_specs = (P("dp", "mp", None), P("dp", "mp"))
    return jax.shard_map(
        per_device, mesh=mesh, in_specs=in_specs, out_specs=out_specs, check_vma=False
    )
```
